256 devices in a mesh: dp: 64 (over z, x, core), seq: 4 (over y).
Axes of the slice: x: 4, y: 4, z: 8, core: 2. Of those that a mesh axis runs over, the one named last changes fastest.
Arguments:
- hidden_in: bfloat16 [65536, 4096], P(('dp', 'seq')), may hold values from -24 to 24
- bc_weight: bfloat16 [4096, 256], P('dp'), may hold values from -0.09375 to 0.09375
- values: bfloat16 [65536, 4096], P(('dp', 'seq')), may hold values from -6 to 6
- teacher: bfloat16 [65536, 4096], P(('dp', 'seq')), may hold values from -6 to 6
- decay_codes: int32 [65536, 64], P(('dp', 'seq')), may hold values from 0 to 15
- resets: int32 [65536], P(('dp', 'seq')), may hold values 0 or 1
- head_decay_rates: float32 [64], replicated, may hold values from 0.25 to 100
- skip_gain: float32 [64], replicated, may hold values from 0.5 to 1.5
- confidence: int32 [65536], P(('dp', 'seq')), may hold values from 1 to 8
Outputs:
- values_grad: bfloat16 [65536, 4096], P(('dp', 'seq'))
- hidden_grad: bfloat16 [65536, 4096], P(('dp', 'seq'))
- weight_grad: float32 [4096, 256], P('dp')
The draws below stay inside these ranges and needn't reach their ends.
All inputs are finite; a program needn't handle non-finite values. No bound on the sum of `resets` on one device may be relied on, other than what follows from the above.
Results may differ from the reference program's by a relative error of at most 0.011.
Values may be sent and summed in bfloat16 or wider, within the bound.
No kernel may reach another device: no remote copies, remote signals or barrier semaphores. Data moves between devices by JAX's collectives and lax.ppermute only.
A program may use at most 128 MiB of HBM per device.

```python
import functools
import math
import jax
import jax.numpy as jnp
from jax import lax

D = 4096
HEADS = 64
HEAD_DIM = 64
STATE = 128
GROUP = 256
DOC_LEN = 1024
DOCS = 64
TOKENS = 65536
INNER = 4096


def draw_head_decay_rates(key, part):
    key_slow = jax.random.fold_in(key, 0)
    return jnp.exp(jax.random.uniform(key_slow, (HEADS,), jnp.float32, math.log(0.25), math.log(100.0)))


def draw_confidence(key, part):
    position = lax.broadcasted_iota(jnp.int32, (TOKENS,), 0) % DOC_LEN
    ceiling = 1 + 8 * position // DOC_LEN
    return jax.random.randint(key, (TOKENS,), 1, ceiling + 1).astype(jnp.int32)


def set_ends(result, key, low, top_value):
    longest = result.shape.index(max(result.shape))
    spots = []
    for shift in (0, 1):
        where = [jax.random.randint(jax.random.fold_in(key, axis), (), 0, length) for axis, length in enumerate(result.shape)]
        where[longest] = (where[longest] + shift) % result.shape[longest]
        spots.append(tuple(where))
    return result.at[spots[0]].set(low).at[spots[1]].set(top_value)


def raised(drawn, rng, source, target, shards_of, factor):
    owner, partner = [(jnp.arange(drawn.shape[dim]) // (drawn.shape[dim] // shards_of)).reshape([-1 if axis == dim else 1 for axis in range(drawn.ndim)]) for dim in (source, target)]
    chosen = jax.random.permutation(rng, shards_of)[partner]
    strong = (owner == chosen) | (owner == (partner + shards_of // 2) % shards_of)
    return jnp.where(strong, factor * drawn, drawn)


def level_of(rng, dims, pieces, smallest, top_value):
    level = 1.0
    for dim, parts in pieces:
        heights = jax.random.uniform(jax.random.fold_in(jax.random.fold_in(rng, 6), dim), (parts,), jnp.float32, smallest / len(pieces), top_value / len(pieces))
        level = level * jnp.repeat(jnp.exp(heights), dims[dim] // parts).reshape((-1,) + (1,) * (len(dims) - 1 - dim))
    return level


def noise(key, shape, deviation, limit, cuts=(), held_as=jnp.bfloat16):
    result = jax.random.normal(key, shape, jnp.float32) * deviation
    if len(cuts) > 0:
        result = level_of(key, shape, cuts, -0.22, 0.18) * result
    return jnp.clip(result, min=-limit, max=limit).astype(held_as)


def heavy_noise(stream_key, extent, scale, limit, shards, heavy, dtype=jnp.bfloat16):
    result = scale * jax.random.normal(stream_key, extent, jnp.float32)
    if shards:
        result = result * level_of(stream_key, extent, shards, -0.22, 0.18)
    return jnp.clip(raised(result, jax.random.fold_in(stream_key, 3), *heavy), -limit, limit).astype(dtype)


def setup_inputs(seed: int = 0) -> dict:
    key_list = jax.random.split(jax.random.key(seed), 10)
    return {
        "hidden_in": heavy_noise(key_list[0], (TOKENS, D), 1.0, 24.0, ((0, 256),), (0, 1, 256, 6.0)),
        "bc_weight": noise(key_list[1], (D, 2 * STATE), D ** -0.5, 0.09375, ((0, 64),)),
        "values": noise(key_list[2], (TOKENS, INNER), 1.0, 6.0, ((0, 256),)),
        "teacher": noise(key_list[3], (TOKENS, INNER), 1.0, 6.0, ((0, 256),)),
        "decay_codes": set_ends(jax.random.randint(key_list[4], (TOKENS, HEADS), 0, 16), jax.random.fold_in(key_list[4], 1), 0, 15).astype(jnp.int32),
        "resets": set_ends((jax.random.randint(key_list[5], (TOKENS,), 0, 128) < 1).astype(jnp.int32), jax.random.fold_in(key_list[5], 1), 0, 1),
        "head_decay_rates": draw_head_decay_rates(jax.random.fold_in(key_list[9], 71), 0),
        "skip_gain": jnp.clip(jax.random.uniform(key_list[7], (HEADS,), jnp.float32, 0.5, 1.5), 0.5, 1.5),
        "confidence": draw_confidence(jax.random.fold_in(key_list[9], 71), 0),
    }


SPIKE_MULTIPLIER = 3000.0
STEP_FACTOR = 16.0

def decay_terms(decay_codes, resets, head_decay_rates):
    logarithm_floor = jnp.log(0.9995 + 0.0004 * decay_codes.astype(jnp.float32) / 15.0)
    decay_logarithm = head_decay_rates[None, :] * (1.0 + SPIKE_MULTIPLIER * resets.astype(jnp.float32))[:, None] * logarithm_floor
    return (decay_logarithm, -STEP_FACTOR * logarithm_floor)

def rounded_value(array):
    return lax.optimization_barrier(array.astype(jnp.bfloat16)).astype(jnp.float32)

def one_document(weight_sum, doc_inputs, bc_weight, head_decay_rates, skip_gain):
    hidden_in, values, teacher, decay_codes, resets, confidence = doc_inputs
    blocks = DOC_LEN // GROUP
    bc_rows = jnp.dot(hidden_in, bc_weight, preferred_element_type=jnp.float32).astype(jnp.bfloat16)
    bc_float = bc_rows.astype(jnp.float32).reshape(blocks, GROUP, 2 * STATE)
    input_map = bc_float[:, :, :STATE]
    output_map = bc_float[:, :, STATE:]
    decay_logarithm, step_size = decay_terms(decay_codes, resets, head_decay_rates)
    cumulative = jnp.cumsum(decay_logarithm.reshape(blocks, GROUP, HEADS), axis=1)
    step_blk = step_size.reshape(blocks, GROUP, HEADS)
    block_log = cumulative[:, -1, :]
    tail_decay = jnp.exp(block_log[:, None, :] - cumulative)
    leading_decay = jnp.exp(cumulative)
    lower_tri = lax.broadcasted_iota(jnp.int32, (GROUP, GROUP), 0) >= lax.broadcasted_iota(jnp.int32, (GROUP, GROUP), 1)
    lower_four = lower_tri[None, :, :, None]
    spread = jnp.where(lower_four, cumulative[:, :, None, :] - cumulative[:, None, :, :], 0.0)
    decay_grid = jnp.where(lower_four, jnp.exp(spread), 0.0) * step_blk[:, None, :, :]
    intersection = jnp.einsum('btn,bsn->bts', output_map, input_map)
    mixing = rounded_value(intersection[..., None] * decay_grid)
    value_blocks = values.astype(jnp.float32).reshape(blocks, GROUP, HEADS, HEAD_DIM)
    write_scale = tail_decay * step_blk
    value_scaled = rounded_value(write_scale[..., None] * value_blocks)
    local_state = jnp.einsum('bshp,bsn->bhpn', value_scaled, input_map)
    zero_state = jnp.zeros((HEADS, HEAD_DIM, STATE), jnp.float32)

    def forward_step(carried, pair):
        step_log, step_state = pair
        return (jnp.exp(step_log)[:, None, None] * carried + step_state, carried)
    _, entry_state = lax.scan(forward_step, zero_state, (block_log, local_state))
    entry_bf = rounded_value(entry_state)
    outputs = jnp.einsum('btsh,bshp->bthp', mixing, value_blocks)
    outputs = outputs + leading_decay[..., None] * jnp.einsum('btn,bhpn->bthp', output_map, entry_bf)
    outputs = outputs + skip_gain[None, None, :, None] * value_blocks
    conf_float = confidence.astype(jnp.float32)
    token_weight = conf_float * DOC_LEN / jnp.sum(conf_float)
    target = teacher.astype(jnp.float32).reshape(blocks, GROUP, HEADS, HEAD_DIM)
    out_grad = rounded_value(token_weight.reshape(blocks, GROUP)[:, :, None, None] * (outputs - target))
    out_scaled = rounded_value(leading_decay[..., None] * out_grad)
    state_pull = jnp.einsum('bthp,btn->bhpn', out_scaled, output_map)

    def backward_step(carried, pair):
        step_log, step_pull = pair
        return (jnp.exp(step_log)[:, None, None] * carried + step_pull, carried)
    _, exit_grad = lax.scan(backward_step, zero_state, (block_log, state_pull), reverse=True)
    exit_bf = rounded_value(exit_grad)
    pair_dots = jnp.einsum('bthp,bshp->btsh', out_grad, value_blocks)
    score_grad = rounded_value(lax.optimization_barrier(jnp.sum(pair_dots * decay_grid, axis=3)))
    values_grad = jnp.einsum('btsh,bthp->bshp', mixing, out_grad)
    values_grad = values_grad + write_scale[..., None] * jnp.einsum('bsn,bhpn->bshp', input_map, exit_bf)
    values_grad = values_grad + skip_gain[None, None, :, None] * out_grad
    input_grad = jnp.einsum('bts,btn->bsn', score_grad, output_map) + jnp.einsum('bshp,bhpn->bsn', value_scaled, exit_bf)
    output_grad = jnp.einsum('bts,bsn->btn', score_grad, input_map) + jnp.einsum('bthp,bhpn->btn', out_scaled, entry_bf)
    bc_grad = jnp.concatenate([input_grad, output_grad], axis=2).reshape(DOC_LEN, 2 * STATE).astype(jnp.bfloat16)
    hidden_grad = jnp.dot(bc_grad, bc_weight.T, preferred_element_type=jnp.float32).astype(jnp.bfloat16)
    weight_sum = weight_sum + jnp.dot(hidden_in.T, bc_grad, preferred_element_type=jnp.float32)
    return (weight_sum, (values_grad.reshape(DOC_LEN, INNER).astype(jnp.bfloat16), hidden_grad))

def reference(hidden_in, bc_weight, values, teacher, decay_codes, resets, head_decay_rates, skip_gain, confidence):
    doc_inputs = (hidden_in.reshape(DOCS, DOC_LEN, D), values.reshape(DOCS, DOC_LEN, INNER), teacher.reshape(DOCS, DOC_LEN, INNER), decay_codes.reshape(DOCS, DOC_LEN, HEADS), resets.reshape(DOCS, DOC_LEN), confidence.reshape(DOCS, DOC_LEN))
    stepper = functools.partial(one_document, bc_weight=bc_weight, head_decay_rates=head_decay_rates, skip_gain=skip_gain)
    weight_sum, grads = lax.scan(stepper, jnp.zeros((D, 2 * STATE), jnp.float32), doc_inputs)
    values_grad = grads[0].reshape(TOKENS, INNER)
    hidden_grad = grads[1].reshape(TOKENS, D)
    return (values_grad, hidden_grad, weight_sum / math.sqrt(TOKENS))
```

```python
import functools
import math

import jax
import jax.numpy as jnp
from jax import lax
from jax.experimental import pallas as pl
from jax.experimental.pallas import tpu as pltpu
from jax.sharding import PartitionSpec as P

BF = jnp.bfloat16
F32 = jnp.float32
BLOCK = 256
HEAD = 64
STATE = 128
PEERS = 4
LOCAL_HEADS = 16
WIDE = LOCAL_HEADS * HEAD
SPIKE_MULTIPLIER = 3000.0
STEP_FACTOR = 16.0
ZREL = (0, 4, 2, 6, 1, 5, 3, 7)
MIB = 1 << 20


def over_dp(x, mask):
    return lax.ppermute(x, "dp", [(i, i ^ mask) for i in range(64)])


def over_seq(x, mask):
    return lax.ppermute(x, "seq", [(i, i ^ mask) for i in range(4)])


def dot_nn(a, b):
    return lax.dot_general(a, b, (((1,), (0,)), ((), ())), preferred_element_type=F32)


def dot_nt(a, b):
    return lax.dot_general(a, b, (((1,), (1,)), ((), ())), preferred_element_type=F32)


def dot_tn(a, b):
    return lax.dot_general(a, b, (((0,), (0,)), ((), ())), preferred_element_type=F32)


def vmem():
    return pl.BlockSpec(memory_space=pltpu.VMEM)


def anywhere():
    return pl.BlockSpec(memory_space=pl.ANY)


def smem():
    return pl.BlockSpec(memory_space=pltpu.SMEM)


def decay_kernel(small_ref, grid_ref, lead_ref, write_ref):
    small = small_ref[0]
    cum_rows = small[0:LOCAL_HEADS]
    step_rows = small[LOCAL_HEADS : 2 * LOCAL_HEADS]
    lead_rows = jnp.exp(cum_rows)
    write_rows = jnp.exp(cum_rows[:, BLOCK - 1 : BLOCK] - cum_rows) * step_rows
    columns = jnp.concatenate([cum_rows, lead_rows, write_rows], axis=0).T
    lower = lax.broadcasted_iota(jnp.int32, (BLOCK, BLOCK), 0) >= lax.broadcasted_iota(
        jnp.int32, (BLOCK, BLOCK), 1
    )
    first = lax.broadcasted_iota(jnp.int32, (BLOCK, 2 * HEAD), 1) < HEAD
    for h in range(LOCAL_HEADS):
        spread = jnp.where(lower, columns[:, h : h + 1] - cum_rows[h : h + 1, :], -1e30)
        grid_ref[0, h] = (jnp.exp(spread) * step_rows[h : h + 1, :]).astype(BF)
    for p in range(LOCAL_HEADS // 2):
        at = slice(2 * HEAD * p, 2 * HEAD * (p + 1))
        for ref, base in ((lead_ref, LOCAL_HEADS), (write_ref, 2 * LOCAL_HEADS)):
            c = base + 2 * p
            ref[0, :, at] = jnp.where(first, columns[:, c : c + 1], columns[:, c + 1 : c + 2])


def decays(small):
    blk = lambda *s: pl.BlockSpec((1, *s), lambda k: (k, *([0] * len(s))))
    return pl.pallas_call(
        decay_kernel,
        grid=(PEERS,),
        in_specs=[blk(*small.shape[1:])],
        out_specs=[blk(LOCAL_HEADS, BLOCK, BLOCK), blk(BLOCK, WIDE), blk(BLOCK, WIDE)],
        out_shape=[
            jax.ShapeDtypeStruct((PEERS, LOCAL_HEADS, BLOCK, BLOCK), BF),
            jax.ShapeDtypeStruct((PEERS, BLOCK, WIDE), F32),
            jax.ShapeDtypeStruct((PEERS, BLOCK, WIDE), F32),
        ],
        compiler_params=pltpu.CompilerParams(vmem_limit_bytes=40 * MIB),
        cost_estimate=pl.CostEstimate(flops=40_000_000, bytes_accessed=17_000_000, transcendentals=4_300_000),
        name="decays",
    )(small)


def turn_kernel(order_ref, core_ref, hidden_ref, out_ref):
    core = core_ref[0]
    turned = hidden_ref[...].T
    out_ref[core, 0] = turned[:HEAD]
    out_ref[1 - core, 0] = turned[HEAD:]


def turn(hidden, order, core):
    return pl.pallas_call(
        turn_kernel,
        grid_spec=pltpu.PrefetchScalarGridSpec(
            num_scalar_prefetch=2,
            grid=(32,),
            in_specs=[pl.BlockSpec((BLOCK, 128), lambda j, order, core: (0, order[j]))],
            out_specs=pl.BlockSpec((2, 1, 64, BLOCK), lambda j, order, core: (0, j, 0, 0)),
        ),
        out_shape=jax.ShapeDtypeStruct((2, 32, 64, BLOCK), BF),
        cost_estimate=pl.CostEstimate(flops=1000, bytes_accessed=4_200_000, transcendentals=0),
        name="turn",
    )(order, core, hidden)


def project_kernel(order_ref, core_ref, hidden_ref, *refs):
    own, other = refs[0:4], refs[4:8]
    weight_ref, rows_ref, sems = refs[8:]
    core = core_ref[0]
    copies = []
    for a in range(4):
        for side, (pieces, place) in enumerate(((own, core), (other, 1 - core))):
            for b in range(8):
                row = pl.multiple_of(order_ref[a * 8 + b] * 128 + place * 64, 64)
                copies.append(
                    pltpu.make_async_copy(
                        pieces[a].at[b], weight_ref.at[pl.ds(row, 64)], sems.at[side, a * 8 + b]
                    )
                )
                copies[-1].start()
    for c in copies:
        c.wait()
    rows_ref[...] = dot_nn(hidden_ref[...], weight_ref[...]).astype(BF)


def project(hidden, own, other, order, core):
    return pl.pallas_call(
        project_kernel,
        in_specs=[smem(), smem(), vmem()] + [anywhere()] * 8,
        out_specs=[vmem(), vmem()],
        out_shape=[
            jax.ShapeDtypeStruct((4096, 256), BF),
            jax.ShapeDtypeStruct((BLOCK, 256), BF),
        ],
        scratch_shapes=[pltpu.SemaphoreType.DMA((2, 32))],
        compiler_params=pltpu.CompilerParams(vmem_limit_bytes=32 * MIB),
        cost_estimate=pl.CostEstimate(flops=540_000_000, bytes_accessed=6_000_000, transcendentals=0),
        name="project",
    )(order, core, hidden, *own, *other)


def layer_kernel(place_ref, *refs):
    xs_in, ts_in, bcs_in = refs[0:4], refs[4:8], refs[8:12]
    grid_in, lead_in, write_in, weight_ref, keep_ref, skip_ref = refs[12:18]
    vg_out, bg_out = refs[18:22], refs[22:26]
    (x, t, bc, grid, lead, write, entry, pull, scaled, outs, acc, state, base, cross, score, ig, sem_a, sem_g) = refs[26:]
    place = place_ref[0]
    first = []
    later = []
    for k in range(PEERS):
        first.append(pltpu.make_async_copy(bcs_in[k], bc.at[k], sem_a.at[0, k]))
        first.append(pltpu.make_async_copy(xs_in[k], x.at[k], sem_a.at[1, k]))
        first.append(pltpu.make_async_copy(write_in.at[k], write.at[k], sem_a.at[2, k]))
    for k in range(PEERS):
        later.append(pltpu.make_async_copy(ts_in[k], t.at[k], sem_a.at[3, k]))
        later.append(pltpu.make_async_copy(lead_in.at[k], lead.at[k], sem_a.at[4, k]))
        later.append(pltpu.make_async_copy(grid_in.at[k], grid.at[k], sem_g.at[k]))
    for c in first + later:
        c.start()
    for c in first:
        c.wait()

    state[...] = jnp.zeros_like(state)
    for j in range(PEERS):
        k = place ^ j
        entry[k] = state[...].astype(BF)
        scaled[k] = (write[k] * x[k].astype(F32)).astype(BF)
        if j < PEERS - 1:
            state[...] = keep_ref[k] * state[...] + dot_tn(bc[k, :, :STATE], scaled[k])
    for c in later:
        c.wait()

    low = lax.broadcasted_iota(jnp.int32, (BLOCK, 2 * HEAD), 1) < HEAD

    def block(k, carry):
        b_map = bc[k, :, :STATE]
        c_map = bc[k, :, STATE:]
        cross[...] = dot_nt(c_map, b_map)
        base[...] = (
            dot_nn(c_map, entry[k]) * lead[k] + skip_ref[...] * x[k].astype(F32) - t[k].astype(F32)
        )
        score[...] = jnp.zeros_like(score)
        weight = weight_ref[k]
        for p in range(LOCAL_HEADS // 2):
            at = slice(2 * HEAD * p, 2 * HEAD * (p + 1))
            xp = x[k, :, at]
            d0 = grid[k, 2 * p].astype(F32)
            d1 = grid[k, 2 * p + 1].astype(F32)
            m0 = (cross[...] * d0).astype(BF)
            m1 = (cross[...] * d1).astype(BF)
            y = jnp.where(low, dot_nn(m0, xp), dot_nn(m1, xp))
            og = (weight * (base[:, at] + y)).astype(BF)
            zero = jnp.zeros_like(og)
            g0 = dot_nt(jnp.where(low, og, zero), xp)
            g1 = dot_nt(jnp.where(low, zero, og), xp)
            score[...] += g0 * d0 + g1 * d1
            dx = jnp.where(low, dot_tn(m0, og), dot_tn(m1, og))
            ogf = og.astype(F32)
            acc[k, :, at] = dx + skip_ref[:, at] * ogf
            outs[:, at] = (lead[k, :, at] * ogf).astype(BF)
        sg = score[...].astype(BF)
        pull[k] = dot_tn(c_map, outs[...])
        ig[k, :, STATE:] = dot_nt(outs[...], entry[k]) + dot_nn(sg, b_map)
        ig[k, :, :STATE] = dot_tn(sg, c_map)
        return carry

    lax.fori_loop(0, PEERS, block, 0)

    state[...] = jnp.zeros_like(state)
    for j in reversed(range(PEERS)):
        k = place ^ j
        leave = state[...].astype(BF)
        acc[k] = acc[k] + write[k] * dot_nn(bc[k, :, :STATE], leave)
        ig[k, :, :STATE] += dot_nt(scaled[k], leave)
        if j > 0:
            state[...] = keep_ref[k] * state[...] + pull[k]
    for k in range(PEERS):
        vg_out[k][...] = acc[k].astype(BF)
        bg_out[k][...] = ig[k].astype(bg_out[k].dtype)


def layer(place, xs, ts, bcs, grid, lead, write, weight, keep, skip):
    return pl.pallas_call(
        layer_kernel,
        in_specs=[smem()] + [anywhere()] * 15 + [vmem()] * 3,
        out_specs=[vmem()] * 8,
        out_shape=[jax.ShapeDtypeStruct((BLOCK, WIDE), BF)] * 4
        + [jax.ShapeDtypeStruct((BLOCK, 2 * STATE), F32)]
        + [jax.ShapeDtypeStruct((BLOCK, 2 * STATE), BF)] * 3,
        scratch_shapes=[
            pltpu.VMEM((PEERS, BLOCK, WIDE), BF),
            pltpu.VMEM((PEERS, BLOCK, WIDE), BF),
            pltpu.VMEM((PEERS, BLOCK, 2 * STATE), BF),
            pltpu.VMEM((PEERS, LOCAL_HEADS, BLOCK, BLOCK), BF),
            pltpu.VMEM((PEERS, BLOCK, WIDE), F32),
            pltpu.VMEM((PEERS, BLOCK, WIDE), F32),
            pltpu.VMEM((PEERS, STATE, WIDE), BF),
            pltpu.VMEM((PEERS, STATE, WIDE), F32),
            pltpu.VMEM((PEERS, BLOCK, WIDE), BF),
            pltpu.VMEM((BLOCK, WIDE), BF),
            pltpu.VMEM((PEERS, BLOCK, WIDE), F32),
            pltpu.VMEM((STATE, WIDE), F32),
            pltpu.VMEM((BLOCK, WIDE), F32),
            pltpu.VMEM((BLOCK, BLOCK), F32),
            pltpu.VMEM((BLOCK, BLOCK), F32),
            pltpu.VMEM((PEERS, BLOCK, 2 * STATE), F32),
            pltpu.SemaphoreType.DMA((5, PEERS)),
            pltpu.SemaphoreType.DMA((PEERS,)),
        ],
        compiler_params=pltpu.CompilerParams(vmem_limit_bytes=56 * MIB),
        cost_estimate=pl.CostEstimate(flops=5_000_000_000, bytes_accessed=24_000_000, transcendentals=0),
        name="layer",
    )(place, *xs, *ts, *bcs, grid, lead, write, weight, keep, skip)


def gather_heads_kernel(place_ref, p0, p1, p2, p3, out_ref, sems):
    copies = []
    for k, piece in enumerate((p0, p1, p2, p3)):
        at = pl.multiple_of((place_ref[0] ^ k) * WIDE, WIDE)
        copies.append(pltpu.make_async_copy(piece, out_ref.at[:, pl.ds(at, WIDE)], sems.at[k]))
        copies[-1].start()
    for c in copies:
        c.wait()


def gather_heads(place, pieces):
    return pl.pallas_call(
        gather_heads_kernel,
        in_specs=[smem()] + [anywhere()] * 4,
        out_specs=anywhere(),
        out_shape=jax.ShapeDtypeStruct((BLOCK, 4 * WIDE), BF),
        scratch_shapes=[pltpu.SemaphoreType.DMA((4,))],
        name="gather_heads",
    )(place, *pieces)


def body(
    hidden_in,
    bc_weight,
    values,
    teacher,
    decay_codes,
    resets,
    head_decay_rates,
    skip_gain,
    confidence,
):
    me = lax.axis_index("seq")
    dp = lax.axis_index("dp")
    place = me.astype(jnp.int32).reshape(1)
    core = (dp % 2).astype(jnp.int32).reshape(1)
    chip = dp // 2
    distance = jnp.array([z * 4 + a for a in range(4) for z in ZREL], jnp.int32)
    order = (chip ^ distance).astype(jnp.int32)
    doc_len = BLOCK * PEERS
    all_tokens = doc_len * 64

    r = bc_weight[None]
    for mask in (32, 16, 8):
        r = jnp.concatenate([r, over_dp(r, mask)], axis=0)
    own = [r] + [over_dp(r, 2 * a) for a in (1, 2, 3)]
    other = [over_dp(p, 1) for p in own]

    def exchange(array):
        cut = [
            lax.dynamic_slice_in_dim(array, (me ^ k) * WIDE, WIDE, axis=1) for k in range(PEERS)
        ]
        return [cut[0]] + [over_seq(cut[k], k) for k in (1, 2, 3)]

    conf_float = confidence.astype(F32)
    base = jnp.log(0.9995 + 0.0004 * decay_codes.astype(F32) / 15.0)
    log_decay = (
        head_decay_rates[None, :] * (1.0 + SPIKE_MULTIPLIER * resets.astype(F32))[:, None] * base
    )
    lower = (
        lax.broadcasted_iota(jnp.int32, (BLOCK, BLOCK), 0)
        >= lax.broadcasted_iota(jnp.int32, (BLOCK, BLOCK), 1)
    ).astype(F32)
    cum_rows = lax.dot_general(
        log_decay, lower, (((0,), (1,)), ((), ())), precision=lax.Precision.HIGHEST
    )
    step_rows = (-STEP_FACTOR * base).T
    packed = jnp.concatenate(
        [
            cum_rows.reshape(PEERS, LOCAL_HEADS, BLOCK),
            step_rows.reshape(PEERS, LOCAL_HEADS, BLOCK),
            jnp.broadcast_to(conf_float[None, None, :], (PEERS, 8, BLOCK)),
        ],
        axis=1,
    )
    cut = [lax.dynamic_index_in_dim(packed, me ^ k, 0, keepdims=False) for k in range(PEERS)]
    small = jnp.stack([cut[0]] + [over_seq(cut[k], k) for k in (1, 2, 3)])
    grid, lead, write = decays(small)
    conf_all = small[:, 2 * LOCAL_HEADS]
    weight = (conf_all * doc_len / jnp.sum(conf_all))[:, :, None]
    keep = jnp.repeat(jnp.exp(small[:, :LOCAL_HEADS, BLOCK - 1]), HEAD, axis=1)[:, None, :]
    skip = jnp.repeat(
        lax.dynamic_slice_in_dim(skip_gain, me * LOCAL_HEADS, LOCAL_HEADS), HEAD
    )[None, :]

    xs = exchange(values)
    ts = exchange(teacher)
    turned = turn(hidden_in, order, core)
    full_weight, rows = project(hidden_in, own, other, order, core)
    bcs = [rows] + [over_seq(rows, k) for k in (1, 2, 3)]

    outs = layer(place, xs, ts, bcs, grid, lead, write, weight, keep, skip)
    vgs, bgs = outs[:4], outs[4:]
    bc_grad = bgs[0]
    for k in (1, 2, 3):
        bc_grad = bc_grad + over_seq(bgs[k], k).astype(F32)
    bc_grad = bc_grad.astype(BF)
    pieces = [vgs[0]] + [over_seq(vgs[k], k) for k in (1, 2, 3)]

    send = dot_nn(turned[1].reshape(2048, BLOCK), bc_grad).astype(BF)
    total = dot_nn(turned[0].reshape(2048, BLOCK), bc_grad)
    total = (total + over_dp(send, 1).astype(F32)).reshape(4, 8, 64, 256)
    came = [over_dp(total[a].astype(BF), 2 * a) for a in (1, 2, 3)]
    total = total[0]
    for c in came:
        total = total + c.astype(F32)
    for mask in (8, 16, 32):
        half = total.shape[0] // 2
        total = total[:half] + over_dp(total[half:].astype(BF), mask).astype(F32)
    total = total[0]
    for mask in (1, 2):
        total = total + over_seq(total, mask)

    hidden_grad = dot_nt(bc_grad, full_weight).astype(BF)
    values_grad = gather_heads(place, pieces)
    return values_grad, hidden_grad, total / math.sqrt(all_tokens)


def solution(mesh):
    return jax.shard_map(
        body,
        mesh=mesh,
        in_specs=(
            P(("dp", "seq"), None),
            P("dp", None),
            P(("dp", "seq"), None),
            P(("dp", "seq"), None),
            P(("dp", "seq"), None),
            P(("dp", "seq")),
            P(),
            P(),
            P(("dp", "seq")),
        ),
        out_specs=(P(("dp", "seq"), None), P(("dp", "seq"), None), P("dp", None)),
        check_vma=False,
    )
```

```python
import functools
import math

import jax
import jax.numpy as jnp
from jax import lax
from jax.experimental import pallas as pl
from jax.experimental.pallas import tpu as pltpu
from jax.sharding import PartitionSpec as P

BF = jnp.bfloat16
F32 = jnp.float32
BLOCK = 256
HEAD = 64
STATE = 128
PEERS = 4
LOCAL_HEADS = 16
WIDE = LOCAL_HEADS * HEAD
SPIKE_MULTIPLIER = 3000.0
STEP_FACTOR = 16.0
ZREL = (0, 4, 2, 6, 1, 5, 3, 7)
MIB = 1 << 20


def over_dp(x, mask):
    return lax.ppermute(x, "dp", [(i, i ^ mask) for i in range(64)])


def over_seq(x, mask):
    return lax.ppermute(x, "seq", [(i, i ^ mask) for i in range(4)])


def dot_nn(a, b):
    return lax.dot_general(a, b, (((1,), (0,)), ((), ())), preferred_element_type=F32)


def dot_nt(a, b):
    return lax.dot_general(a, b, (((1,), (1,)), ((), ())), preferred_element_type=F32)


def dot_tn(a, b):
    return lax.dot_general(a, b, (((0,), (0,)), ((), ())), preferred_element_type=F32)


def vmem():
    return pl.BlockSpec(memory_space=pltpu.VMEM)


def anywhere():
    return pl.BlockSpec(memory_space=pl.ANY)


def smem():
    return pl.BlockSpec(memory_space=pltpu.SMEM)


def after(arrays, waits):
    n = len(arrays)
    return pl.pallas_call(
        lambda *refs: None,
        in_specs=[anywhere()] * (n + len(waits)),
        out_specs=[anywhere()] * n,
        out_shape=[jax.ShapeDtypeStruct(a.shape, a.dtype) for a in arrays],
        input_output_aliases={i: i for i in range(n)},
        name="after",
    )(*arrays, *waits)


def decay_kernel(small_ref, grid_ref, lead_ref, write_ref, done_ref):
    done_ref[...] = jnp.zeros_like(done_ref)
    small = small_ref[0]
    cum_rows = small[0:LOCAL_HEADS]
    step_rows = small[LOCAL_HEADS : 2 * LOCAL_HEADS]
    lead_rows = jnp.exp(cum_rows)
    write_rows = jnp.exp(cum_rows[:, BLOCK - 1 : BLOCK] - cum_rows) * step_rows
    columns = jnp.concatenate([cum_rows, lead_rows, write_rows], axis=0).T
    lower = lax.broadcasted_iota(jnp.int32, (BLOCK, BLOCK), 0) >= lax.broadcasted_iota(
        jnp.int32, (BLOCK, BLOCK), 1
    )
    first = lax.broadcasted_iota(jnp.int32, (BLOCK, 2 * HEAD), 1) < HEAD
    for h in range(LOCAL_HEADS):
        spread = jnp.where(lower, columns[:, h : h + 1] - cum_rows[h : h + 1, :], -1e30)
        grid_ref[0, h] = (jnp.exp(spread) * step_rows[h : h + 1, :]).astype(BF)
    for p in range(LOCAL_HEADS // 2):
        at = slice(2 * HEAD * p, 2 * HEAD * (p + 1))
        for ref, base in ((lead_ref, LOCAL_HEADS), (write_ref, 2 * LOCAL_HEADS)):
            c = base + 2 * p
            both = jnp.where(first, columns[:, c : c + 1], columns[:, c + 1 : c + 2])
            ref[0, :, at] = both.astype(BF)


def decays(small):
    blk = lambda *s: pl.BlockSpec((1, *s), lambda k: (k, *([0] * len(s))))
    return pl.pallas_call(
        decay_kernel,
        grid=(PEERS,),
        in_specs=[blk(*small.shape[1:])],
        out_specs=[blk(LOCAL_HEADS, BLOCK, BLOCK), blk(BLOCK, WIDE), blk(BLOCK, WIDE), pl.BlockSpec((8, 128), lambda k: (0, 0))],
        out_shape=[
            jax.ShapeDtypeStruct((PEERS, LOCAL_HEADS, BLOCK, BLOCK), BF),
            jax.ShapeDtypeStruct((PEERS, BLOCK, WIDE), BF),
            jax.ShapeDtypeStruct((PEERS, BLOCK, WIDE), BF),
            jax.ShapeDtypeStruct((8, 128), F32),
        ],
        compiler_params=pltpu.CompilerParams(vmem_limit_bytes=16 * MIB),
        cost_estimate=pl.CostEstimate(flops=40_000_000, bytes_accessed=17_000_000, transcendentals=4_300_000),
        name="decays",
    )(small)


def cut_heads_kernel(place_ref, values_ref, aux_ref, teacher_ref, *refs):
    v_outs, t_outs, sems = refs[0:3], refs[3:6], refs[6]
    copies = []
    for k in (1, 2, 3):
        to = place_ref[0] ^ k
        wide = pl.ds(pl.multiple_of(to * WIDE, WIDE), WIDE)
        thin = pl.ds(pl.multiple_of(to * 128, 128), 128)
        for n, (src, dst) in enumerate(
            (
                (values_ref.at[:, wide], v_outs[k - 1].at[:, pl.ds(0, WIDE)]),
                (aux_ref.at[:, thin], v_outs[k - 1].at[:, pl.ds(WIDE, 128)]),
                (teacher_ref.at[:, wide], t_outs[k - 1]),
            )
        ):
            copies.append(pltpu.make_async_copy(src, dst, sems.at[n, k]))
            copies[-1].start()
    for c in copies:
        c.wait()


def cut_heads(place, values, aux, teacher):
    return pl.pallas_call(
        cut_heads_kernel,
        in_specs=[smem()] + [anywhere()] * 3,
        out_specs=[vmem()] * 6,
        out_shape=[jax.ShapeDtypeStruct((BLOCK, WIDE + 128), BF)] * 3
        + [jax.ShapeDtypeStruct((BLOCK, WIDE), BF)] * 3,
        scratch_shapes=[pltpu.SemaphoreType.DMA((3, 4))],
        cost_estimate=pl.CostEstimate(flops=1000, bytes_accessed=6_400_000, transcendentals=0),
        name="cut_heads",
    )(place, values, aux, teacher)


def split_hidden_kernel(x_ref, hidden_ref, *refs):
    outs, done_ref, sems = refs[:4], refs[4], refs[5]
    done_ref[...] = jnp.zeros_like(done_ref)
    copies = []
    for a in range(4):
        for z in range(8):
            at = pl.multiple_of((z * 4 + (x_ref[0] ^ a)) * 128, 128)
            copies.append(
                pltpu.make_async_copy(
                    hidden_ref.at[:, pl.ds(at, 128)],
                    outs[a].at[:, pl.ds(128 * z, 128)],
                    sems.at[a, z],
                )
            )
            copies[-1].start()
    for c in copies:
        c.wait()


def split_hidden(x, hidden):
    return pl.pallas_call(
        split_hidden_kernel,
        in_specs=[smem(), anywhere()],
        out_specs=[vmem()] * 5,
        out_shape=[jax.ShapeDtypeStruct((BLOCK, 1024), BF)] * 4 + [jax.ShapeDtypeStruct((8, 128), F32)],
        scratch_shapes=[pltpu.SemaphoreType.DMA((4, 8))],
        cost_estimate=pl.CostEstimate(flops=1000, bytes_accessed=4_200_000, transcendentals=0),
        name="split_hidden",
    )(x, hidden)


def turn_kernel(pos_ref, core_ref, p0, p1, p2, p3, out_ref):
    core = core_ref[0]
    for z in range(8):
        for a, piece in enumerate((p0, p1, p2, p3)):
            turned = piece[:, 128 * z : 128 * (z + 1)].T
            at = slice(BLOCK * a, BLOCK * (a + 1))
            out_ref[core, pos_ref[z], :, at] = turned[:HEAD]
            out_ref[1 - core, pos_ref[z], :, at] = turned[HEAD:]


def turn(pos, core, pieces):
    return pl.pallas_call(
        turn_kernel,
        in_specs=[smem(), smem()] + [vmem()] * 4,
        out_specs=vmem(),
        out_shape=jax.ShapeDtypeStruct((2, 8, 64, 4 * BLOCK), BF),
        compiler_params=pltpu.CompilerParams(vmem_limit_bytes=14 * MIB),
        cost_estimate=pl.CostEstimate(flops=1000, bytes_accessed=14_000_000, transcendentals=0),
        name="turn",
    )(pos, core, *pieces)


def project_kernel(order_ref, core_ref, hidden_ref, *refs):
    own, other = refs[0:4], refs[4:8]
    weight_ref, rows_ref, sems = refs[-3:]
    core = core_ref[0]
    copies = []
    for side, (pieces, place) in enumerate(((own, core), (other, 1 - core))):
        for a in range(4):
            for b in range(8):
                row = pl.multiple_of(order_ref[a * 8 + b] * 128 + place * 64, 64)
                copies.append(
                    pltpu.make_async_copy(
                        pieces[a].at[b], weight_ref.at[pl.ds(row, 64)], sems.at[side, a * 8 + b]
                    )
                )
                copies[-1].start()
    for c in copies:
        c.wait()
    rows_ref[...] = dot_nn(hidden_ref[...], weight_ref[...]).astype(BF)


def project(hidden, own, other, order, core, waits):
    return pl.pallas_call(
        project_kernel,
        in_specs=[smem(), smem(), vmem()] + [anywhere()] * (8 + len(waits)),
        out_specs=[vmem(), vmem()],
        out_shape=[
            jax.ShapeDtypeStruct((4096, 256), BF),
            jax.ShapeDtypeStruct((BLOCK, 256), BF),
        ],
        scratch_shapes=[pltpu.SemaphoreType.DMA((2, 32))],
        compiler_params=pltpu.CompilerParams(vmem_limit_bytes=14 * MIB),
        cost_estimate=pl.CostEstimate(flops=540_000_000, bytes_accessed=6_000_000, transcendentals=0),
        name="project",
    )(order, core, hidden, *own, *other, *waits)


def layer_kernel(place_ref, *refs):
    xs_in, ts_in, bcs_in = refs[0:4], refs[4:8], refs[8:12]
    grid_in, lead_in, write_in, weight_ref, keep_ref, skip_ref = refs[12:18]
    vg_out, bg_out = refs[18:22], refs[22:26]
    (x, t, bc, grid, lead, write, entry, pull, scaled, outs, acc, state, base, cross, score, ig, sem_a, sem_g) = refs[26:]
    place = place_ref[0]
    first = []
    later = [[] for _ in range(PEERS)]
    for k in range(PEERS):
        first.append(pltpu.make_async_copy(bcs_in[k], bc.at[k], sem_a.at[0, k]))
        own = pl.ds(pl.multiple_of(place * WIDE, WIDE), WIDE)
        x_in = xs_in[k].at[:, own if k == 0 else pl.ds(0, WIDE)]
        first.append(pltpu.make_async_copy(x_in, x.at[k], sem_a.at[1, k]))
        first.append(pltpu.make_async_copy(write_in.at[k], write.at[k], sem_a.at[2, k]))
    for k in range(PEERS):
        t_in = ts_in[k].at[:, own] if k == 0 else ts_in[k]
        later[k].append(pltpu.make_async_copy(t_in, t.at[k], sem_a.at[3, k]))
        later[k].append(pltpu.make_async_copy(lead_in.at[k], lead.at[k], sem_a.at[4, k]))
        later[k].append(pltpu.make_async_copy(grid_in.at[k], grid.at[k], sem_g.at[k]))
    for c in first + sum(later, []):
        c.start()
    for c in first:
        c.wait()

    state[...] = jnp.zeros_like(state)
    for j in range(PEERS):
        k = place ^ j
        entry[k] = state[...].astype(BF)
        scaled[k] = (write[k].astype(F32) * x[k].astype(F32)).astype(BF)
        if j < PEERS - 1:
            state[...] = keep_ref[k] * state[...] + dot_tn(bc[k, :, :STATE], scaled[k])
    low = lax.broadcasted_iota(jnp.int32, (BLOCK, 2 * HEAD), 1) < HEAD

    def block(k, carry):
        for ref, sem in ((t, sem_a.at[3, k]), (lead, sem_a.at[4, k]), (grid, sem_g.at[k])):
            pltpu.make_async_copy(ref.at[k], ref.at[k], sem).wait()
        b_map = bc[k, :, :STATE]
        c_map = bc[k, :, STATE:]
        cross[...] = dot_nt(c_map, b_map)
        base[...] = (
            dot_nn(c_map, entry[k]) * lead[k].astype(F32) + skip_ref[...] * x[k].astype(F32) - t[k].astype(F32)
        )
        score[...] = jnp.zeros_like(score)
        weight = weight_ref[k]
        for p in range(LOCAL_HEADS // 2):
            at = slice(2 * HEAD * p, 2 * HEAD * (p + 1))
            xp = x[k, :, at]
            d0 = grid[k, 2 * p].astype(F32)
            d1 = grid[k, 2 * p + 1].astype(F32)
            m0 = (cross[...] * d0).astype(BF)
            m1 = (cross[...] * d1).astype(BF)
            y = jnp.where(low, dot_nn(m0, xp), dot_nn(m1, xp))
            og = (weight * (base[:, at] + y)).astype(BF)
            zero = jnp.zeros_like(og)
            g0 = dot_nt(jnp.where(low, og, zero), xp)
            g1 = dot_nt(jnp.where(low, zero, og), xp)
            score[...] += g0 * d0 + g1 * d1
            dx = jnp.where(low, dot_tn(m0, og), dot_tn(m1, og))
            ogf = og.astype(F32)
            acc[k, :, at] = dx + skip_ref[:, at] * ogf
            outs[:, at] = (lead[k, :, at].astype(F32) * ogf).astype(BF)
        sg = score[...].astype(BF)
        pull[k] = dot_tn(c_map, outs[...])
        ig[k, :, STATE:] = dot_nt(outs[...], entry[k]) + dot_nn(sg, b_map)
        ig[k, :, :STATE] = dot_tn(sg, c_map)
        return carry

    lax.fori_loop(0, PEERS, block, 0)

    state[...] = jnp.zeros_like(state)
    for j in reversed(range(PEERS)):
        k = place ^ j
        leave = state[...].astype(BF)
        acc[k] = acc[k] + write[k].astype(F32) * dot_nn(bc[k, :, :STATE], leave)
        ig[k, :, :STATE] += dot_nt(scaled[k], leave)
        if j > 0:
            state[...] = keep_ref[k] * state[...] + pull[k]
    for k in range(PEERS):
        vg_out[k][...] = acc[k].astype(BF)
        bg_out[k][...] = ig[k].astype(bg_out[k].dtype)


def layer(place, xs, ts, bcs, grid, lead, write, weight, keep, skip):
    return pl.pallas_call(
        layer_kernel,
        in_specs=[smem()] + [anywhere()] * 15 + [vmem()] * 3,
        out_specs=[vmem()] * 8,
        out_shape=[jax.ShapeDtypeStruct((BLOCK, WIDE), BF)] * 4
        + [jax.ShapeDtypeStruct((BLOCK, 2 * STATE), F32)]
        + [jax.ShapeDtypeStruct((BLOCK, 2 * STATE), BF)] * 3,
        scratch_shapes=[
            pltpu.VMEM((PEERS, BLOCK, WIDE), BF),
            pltpu.VMEM((PEERS, BLOCK, WIDE), BF),
            pltpu.VMEM((PEERS, BLOCK, 2 * STATE), BF),
            pltpu.VMEM((PEERS, LOCAL_HEADS, BLOCK, BLOCK), BF),
            pltpu.VMEM((PEERS, BLOCK, WIDE), BF),
            pltpu.VMEM((PEERS, BLOCK, WIDE), BF),
            pltpu.VMEM((PEERS, STATE, WIDE), BF),
            pltpu.VMEM((PEERS, STATE, WIDE), F32),
            pltpu.VMEM((PEERS, BLOCK, WIDE), BF),
            pltpu.VMEM((BLOCK, WIDE), BF),
            pltpu.VMEM((PEERS, BLOCK, WIDE), F32),
            pltpu.VMEM((STATE, WIDE), F32),
            pltpu.VMEM((BLOCK, WIDE), F32),
            pltpu.VMEM((BLOCK, BLOCK), F32),
            pltpu.VMEM((BLOCK, BLOCK), F32),
            pltpu.VMEM((PEERS, BLOCK, 2 * STATE), F32),
            pltpu.SemaphoreType.DMA((5, PEERS)),
            pltpu.SemaphoreType.DMA((PEERS,)),
        ],
        compiler_params=pltpu.CompilerParams(vmem_limit_bytes=56 * MIB),
        cost_estimate=pl.CostEstimate(flops=5_000_000_000, bytes_accessed=24_000_000, transcendentals=0),
        name="layer",
    )(place, *xs, *ts, *bcs, grid, lead, write, weight, keep, skip)


def gather_heads_kernel(place_ref, p0, p1, p2, p3, out_ref, sems):
    copies = []
    for k, piece in enumerate((p0, p1, p2, p3)):
        at = pl.multiple_of((place_ref[0] ^ k) * WIDE, WIDE)
        copies.append(pltpu.make_async_copy(piece, out_ref.at[:, pl.ds(at, WIDE)], sems.at[k]))
        copies[-1].start()
    for c in copies:
        c.wait()


def gather_heads(place, pieces):
    return pl.pallas_call(
        gather_heads_kernel,
        in_specs=[smem()] + [anywhere()] * 4,
        out_specs=vmem(),
        out_shape=jax.ShapeDtypeStruct((BLOCK, 4 * WIDE), BF),
        scratch_shapes=[pltpu.SemaphoreType.DMA((4,))],
        cost_estimate=pl.CostEstimate(flops=1000, bytes_accessed=4_200_000, transcendentals=0),
        name="gather_heads",
    )(place, *pieces)


def body(
    hidden_in,
    bc_weight,
    values,
    teacher,
    decay_codes,
    resets,
    head_decay_rates,
    skip_gain,
    confidence,
):
    me = lax.axis_index("seq")
    dp = lax.axis_index("dp")
    place = me.astype(jnp.int32).reshape(1)
    core = (dp % 2).astype(jnp.int32).reshape(1)
    chip = dp // 2
    distance = jnp.array([z * 4 + a for a in range(4) for z in ZREL], jnp.int32)
    order = (chip ^ distance).astype(jnp.int32)
    x_place = (chip % 4).astype(jnp.int32).reshape(1)
    turns = jnp.array([ZREL.index(z) for z in range(8)], jnp.int32)
    pos = turns[jnp.arange(8, dtype=jnp.int32) ^ (chip // 4)]
    doc_len = BLOCK * PEERS
    all_tokens = doc_len * 64

    aux = jnp.concatenate(
        [
            decay_codes.astype(BF).reshape(BLOCK, PEERS, LOCAL_HEADS),
            jnp.broadcast_to(resets.astype(BF)[:, None, None], (BLOCK, PEERS, 1)),
            jnp.broadcast_to(confidence.astype(BF)[:, None, None], (BLOCK, PEERS, 1)),
            jnp.zeros((BLOCK, PEERS, 128 - LOCAL_HEADS - 2), BF),
        ],
        axis=2,
    ).reshape(BLOCK, PEERS * 128)
    cut = cut_heads(place, values, aux, teacher)
    v_cut, t_cut = cut[0:3], cut[3:6]
    x1, x3 = over_seq(v_cut[0], 1), over_seq(v_cut[2], 3)
    (far,) = after([v_cut[1]], [x1])
    xs = [values, x1, over_seq(far, 2), x3]
    near = after([t_cut[0], t_cut[2]], [x3])
    ts = [teacher, over_seq(near[0], 1), over_seq(t_cut[1], 2), over_seq(near[1], 3)]

    facts = jnp.stack(
        [lax.dynamic_slice_in_dim(aux, me * 128, 128, axis=1)] + [x[:, WIDE:] for x in xs[1:]]
    ).astype(F32)
    base = jnp.log(0.9995 + 0.0004 * facts[:, :, :LOCAL_HEADS] / 15.0)
    rates = lax.dynamic_slice_in_dim(head_decay_rates, me * LOCAL_HEADS, LOCAL_HEADS)
    log_decay = (
        rates[None, None, :] * (1.0 + SPIKE_MULTIPLIER * facts[:, :, LOCAL_HEADS, None]) * base
    )
    lower = (
        lax.broadcasted_iota(jnp.int32, (BLOCK, BLOCK), 0)
        >= lax.broadcasted_iota(jnp.int32, (BLOCK, BLOCK), 1)
    ).astype(F32)
    cum_rows = jnp.swapaxes(
        jnp.einsum("ts,ksh->kth", lower, log_decay, precision=lax.Precision.HIGHEST), 1, 2
    )
    step_rows = jnp.swapaxes(-STEP_FACTOR * base, 1, 2)
    small = jnp.concatenate([cum_rows, step_rows], axis=1)
    grid, lead, write, decayed = decays(small)
    conf_all = facts[:, :, LOCAL_HEADS + 1]
    weight = (conf_all * doc_len / jnp.sum(conf_all))[:, :, None]
    keep = jnp.repeat(jnp.exp(small[:, :LOCAL_HEADS, BLOCK - 1]), HEAD, axis=1)[:, None, :]
    skip = jnp.repeat(
        lax.dynamic_slice_in_dim(skip_gain, me * LOCAL_HEADS, LOCAL_HEADS), HEAD
    )[None, :]

    r = bc_weight[None]
    r = jnp.concatenate([r, over_dp(r, 32)], axis=0)
    r = jnp.concatenate([r] + [over_dp(r, m) for m in (16, 8, 24)], axis=0)
    (r,) = after([r], [xs[1], xs[3]])
    own = [r] + [over_dp(r, 2 * a) for a in (1, 2, 3)]
    other = [over_dp(p, 1) for p in own]
    full_weight, rows = project(hidden_in, own, other, order, core, [decayed])
    (rows,) = after([rows], [ts[1], ts[3]])
    *hx, cut_done = split_hidden(x_place, hidden_in)
    bcs = [rows] + [over_seq(rows, k) for k in (1, 2, 3)]
    near = after([hx[1], hx[3]], [own[3]])
    hx1, hx3 = over_dp(near[0], 2), over_dp(near[1], 6)
    hx = [hx[0], hx1, over_dp(hx[2], 4), hx3]
    (bcs[0],) = after([bcs[0]], [hx1])

    outs = layer(place, xs, ts, bcs, grid, lead, write, weight, keep, skip)
    vgs, bgs = outs[:4], outs[4:]
    bc_grad = bgs[0]
    for k in (1, 2, 3):
        bc_grad = bc_grad + over_seq(bgs[k], k).astype(F32)
    bc_grad = bc_grad.astype(BF)
    pieces = [vgs[0]] + [over_seq(vgs[k], k) for k in (1, 2, 3)]

    bc_grads = jnp.concatenate([bc_grad] + [over_dp(bc_grad, 2 * a) for a in (1, 2, 3)], axis=0)
    turned = turn(pos, core, hx)
    send = dot_nn(turned[1].reshape(512, 4 * BLOCK), bc_grads).astype(BF)
    (send,) = after([send], [pieces[1], pieces[3]])
    total = dot_nn(turned[0].reshape(512, 4 * BLOCK), bc_grads)
    total = (total + over_dp(send, 1).astype(F32)).reshape(8, 64, 256)
    half = total.astype(BF)
    came = [over_dp(half[2:4], 16), over_dp(half[4:6], 8), over_dp(half[6:8], 24)]
    total = total[0:2]
    for c in came:
        total = total + c.astype(F32)
    (total,) = after([total], [pieces[2]])
    total = total[0] + over_dp(total[1].astype(BF), 32).astype(F32)

    hidden_grad = dot_nt(bc_grad, full_weight).astype(BF)
    values_grad = gather_heads(place, pieces)
    total = total + sum(over_seq(total, k) for k in (1, 2, 3))
    return values_grad, hidden_grad, total / math.sqrt(all_tokens)


def solution(mesh):
    return jax.shard_map(
        body,
        mesh=mesh,
        in_specs=(
            P(("dp", "seq"), None),
            P("dp", None),
            P(("dp", "seq"), None),
            P(("dp", "seq"), None),
            P(("dp", "seq"), None),
            P(("dp", "seq")),
            P(),
            P(),
            P(("dp", "seq")),
        ),
        out_specs=(P(("dp", "seq"), None), P(("dp", "seq"), None), P("dp", None)),
        check_vma=False,
    )
```

```python
import functools
import math

import jax
import jax.numpy as jnp
from jax import lax
from jax.experimental import pallas as pl
from jax.experimental.pallas import tpu as pltpu
from jax.sharding import PartitionSpec as P

BF = jnp.bfloat16
F32 = jnp.float32
BLOCK = 256
HEAD = 64
STATE = 128
PEERS = 4
LOCAL_HEADS = 16
WIDE = LOCAL_HEADS * HEAD
SPIKE_MULTIPLIER = 3000.0
STEP_FACTOR = 16.0
ZREL = (0, 4, 2, 6, 1, 5, 3, 7)
MIB = 1 << 20


def over_dp(x, mask):
    return lax.ppermute(x, "dp", [(i, i ^ mask) for i in range(64)])


def over_seq(x, mask):
    return lax.ppermute(x, "seq", [(i, i ^ mask) for i in range(4)])


def dot_nn(a, b):
    return lax.dot_general(a, b, (((1,), (0,)), ((), ())), preferred_element_type=F32)


def dot_nt(a, b):
    return lax.dot_general(a, b, (((1,), (1,)), ((), ())), preferred_element_type=F32)


def dot_tn(a, b):
    return lax.dot_general(a, b, (((0,), (0,)), ((), ())), preferred_element_type=F32)


def vmem():
    return pl.BlockSpec(memory_space=pltpu.VMEM)


def anywhere():
    return pl.BlockSpec(memory_space=pl.ANY)


def smem():
    return pl.BlockSpec(memory_space=pltpu.SMEM)


def after(arrays, waits):
    n = len(arrays)
    return pl.pallas_call(
        lambda *refs: None,
        in_specs=[anywhere()] * (n + len(waits)),
        out_specs=[anywhere()] * n,
        out_shape=[jax.ShapeDtypeStruct(a.shape, a.dtype) for a in arrays],
        input_output_aliases={i: i for i in range(n)},
        name="after",
    )(*arrays, *waits)


def decay_kernel(small_ref, grid_ref, lead_ref, write_ref, done_ref):
    done_ref[...] = jnp.zeros_like(done_ref)
    small = small_ref[0]
    cum_rows = small[0:LOCAL_HEADS]
    step_rows = small[LOCAL_HEADS : 2 * LOCAL_HEADS]
    lead_rows = jnp.exp(cum_rows)
    write_rows = jnp.exp(cum_rows[:, BLOCK - 1 : BLOCK] - cum_rows) * step_rows
    columns = jnp.concatenate([cum_rows, lead_rows, write_rows], axis=0).T
    lower = lax.broadcasted_iota(jnp.int32, (BLOCK, BLOCK), 0) >= lax.broadcasted_iota(
        jnp.int32, (BLOCK, BLOCK), 1
    )
    first = lax.broadcasted_iota(jnp.int32, (BLOCK, 2 * HEAD), 1) < HEAD
    for h in range(LOCAL_HEADS):
        spread = jnp.where(lower, columns[:, h : h + 1] - cum_rows[h : h + 1, :], -1e30)
        grid_ref[0, h] = (jnp.exp(spread) * step_rows[h : h + 1, :]).astype(BF)
    for p in range(LOCAL_HEADS // 2):
        at = slice(2 * HEAD * p, 2 * HEAD * (p + 1))
        for ref, base in ((lead_ref, LOCAL_HEADS), (write_ref, 2 * LOCAL_HEADS)):
            c = base + 2 * p
            both = jnp.where(first, columns[:, c : c + 1], columns[:, c + 1 : c + 2])
            ref[0, :, at] = both.astype(BF)


def decays(small):
    blk = lambda *s: pl.BlockSpec((1, *s), lambda k: (k, *([0] * len(s))))
    return pl.pallas_call(
        decay_kernel,
        grid=(PEERS,),
        in_specs=[blk(*small.shape[1:])],
        out_specs=[blk(LOCAL_HEADS, BLOCK, BLOCK), blk(BLOCK, WIDE), blk(BLOCK, WIDE), pl.BlockSpec((8, 128), lambda k: (0, 0))],
        out_shape=[
            jax.ShapeDtypeStruct((PEERS, LOCAL_HEADS, BLOCK, BLOCK), BF),
            jax.ShapeDtypeStruct((PEERS, BLOCK, WIDE), BF),
            jax.ShapeDtypeStruct((PEERS, BLOCK, WIDE), BF),
            jax.ShapeDtypeStruct((8, 128), F32),
        ],
        compiler_params=pltpu.CompilerParams(vmem_limit_bytes=16 * MIB),
        cost_estimate=pl.CostEstimate(flops=40_000_000, bytes_accessed=17_000_000, transcendentals=4_300_000),
        name="decays",
    )(small)


def cut_heads_kernel(place_ref, values_ref, aux_ref, teacher_ref, wait_ref, *refs):
    v_outs, t_outs, sems = refs[0:3], refs[3:6], refs[6]
    copies = []
    for k in (1, 2, 3):
        to = place_ref[0] ^ k
        wide = pl.ds(pl.multiple_of(to * WIDE, WIDE), WIDE)
        thin = pl.ds(pl.multiple_of(to * 128, 128), 128)
        for n, (src, dst) in enumerate(
            (
                (values_ref.at[:, wide], v_outs[k - 1].at[:, pl.ds(0, WIDE)]),
                (aux_ref.at[:, thin], v_outs[k - 1].at[:, pl.ds(WIDE, 128)]),
                (teacher_ref.at[:, wide], t_outs[k - 1]),
            )
        ):
            copies.append(pltpu.make_async_copy(src, dst, sems.at[n, k]))
            copies[-1].start()
    for c in copies:
        c.wait()


def cut_heads(place, values, aux, teacher, wait):
    return pl.pallas_call(
        cut_heads_kernel,
        in_specs=[smem()] + [anywhere()] * 4,
        out_specs=[vmem()] * 6,
        out_shape=[jax.ShapeDtypeStruct((BLOCK, WIDE + 128), BF)] * 3
        + [jax.ShapeDtypeStruct((BLOCK, WIDE), BF)] * 3,
        scratch_shapes=[pltpu.SemaphoreType.DMA((3, 4))],
        cost_estimate=pl.CostEstimate(flops=1000, bytes_accessed=6_400_000, transcendentals=0),
        name="cut_heads",
    )(place, values, aux, teacher, wait)


def split_hidden_kernel(x_ref, hidden_ref, wait_ref, *refs):
    outs, done_ref, sems = refs[:4], refs[4], refs[5]
    done_ref[...] = jnp.zeros_like(done_ref)
    copies = []
    for a in range(4):
        for z in range(8):
            at = pl.multiple_of((z * 4 + (x_ref[0] ^ a)) * 128, 128)
            copies.append(
                pltpu.make_async_copy(
                    hidden_ref.at[:, pl.ds(at, 128)],
                    outs[a].at[:, pl.ds(128 * z, 128)],
                    sems.at[a, z],
                )
            )
            copies[-1].start()
    for c in copies:
        c.wait()


def split_hidden(x, hidden, wait):
    return pl.pallas_call(
        split_hidden_kernel,
        in_specs=[smem(), anywhere(), anywhere()],
        out_specs=[vmem()] * 5,
        out_shape=[jax.ShapeDtypeStruct((BLOCK, 1024), BF)] * 4 + [jax.ShapeDtypeStruct((8, 128), F32)],
        scratch_shapes=[pltpu.SemaphoreType.DMA((4, 8))],
        cost_estimate=pl.CostEstimate(flops=1000, bytes_accessed=4_200_000, transcendentals=0),
        name="split_hidden",
    )(x, hidden, wait)


def turn_kernel(pos_ref, core_ref, p0, p1, p2, p3, out_ref):
    core = core_ref[0]
    for z in range(8):
        for a, piece in enumerate((p0, p1, p2, p3)):
            turned = piece[:, 128 * z : 128 * (z + 1)].T
            at = slice(BLOCK * a, BLOCK * (a + 1))
            out_ref[core, pos_ref[z], :, at] = turned[:HEAD]
            out_ref[1 - core, pos_ref[z], :, at] = turned[HEAD:]


def turn(pos, core, pieces):
    return pl.pallas_call(
        turn_kernel,
        in_specs=[smem(), smem()] + [vmem()] * 4,
        out_specs=vmem(),
        out_shape=jax.ShapeDtypeStruct((2, 8, 64, 4 * BLOCK), BF),
        compiler_params=pltpu.CompilerParams(vmem_limit_bytes=14 * MIB),
        cost_estimate=pl.CostEstimate(flops=1000, bytes_accessed=14_000_000, transcendentals=0),
        name="turn",
    )(pos, core, *pieces)


def project_kernel(order_ref, core_ref, hidden_ref, *refs):
    own, other = refs[0:4], refs[4:8]
    weight_ref, rows_ref, sems = refs[-3:]
    core = core_ref[0]
    copies = []
    for side, (pieces, place) in enumerate(((own, core), (other, 1 - core))):
        for a in range(4):
            for b in range(8):
                row = pl.multiple_of(order_ref[a * 8 + b] * 128 + place * 64, 64)
                copies.append(
                    pltpu.make_async_copy(
                        pieces[a].at[b], weight_ref.at[pl.ds(row, 64)], sems.at[side, a * 8 + b]
                    )
                )
                copies[-1].start()
    for c in copies:
        c.wait()
    rows_ref[...] = dot_nn(hidden_ref[...], weight_ref[...]).astype(BF)


def project(hidden, own, other, order, core, waits):
    return pl.pallas_call(
        project_kernel,
        in_specs=[smem(), smem(), vmem()] + [anywhere()] * (8 + len(waits)),
        out_specs=[vmem(), vmem()],
        out_shape=[
            jax.ShapeDtypeStruct((4096, 256), BF),
            jax.ShapeDtypeStruct((BLOCK, 256), BF),
        ],
        scratch_shapes=[pltpu.SemaphoreType.DMA((2, 32))],
        compiler_params=pltpu.CompilerParams(vmem_limit_bytes=14 * MIB),
        cost_estimate=pl.CostEstimate(flops=540_000_000, bytes_accessed=6_000_000, transcendentals=0),
        name="project",
    )(order, core, hidden, *own, *other, *waits)


def layer_kernel(place_ref, *refs):
    xs_in, ts_in, bcs_in = refs[0:4], refs[4:8], refs[8:12]
    grid_in, lead_in, write_in, weight_ref, keep_ref, skip_ref = refs[12:18]
    vg_out, bg_out = refs[18:22], refs[22:26]
    (x, t, bc, grid, lead, write, entry, pull, scaled, outs, acc, state, base, cross, score, ig, sem_a, sem_g) = refs[26:]
    place = place_ref[0]
    first = []
    later = [[] for _ in range(PEERS)]
    for k in range(PEERS):
        first.append(pltpu.make_async_copy(bcs_in[k], bc.at[k], sem_a.at[0, k]))
        own = pl.ds(pl.multiple_of(place * WIDE, WIDE), WIDE)
        x_in = xs_in[k].at[:, own if k == 0 else pl.ds(0, WIDE)]
        first.append(pltpu.make_async_copy(x_in, x.at[k], sem_a.at[1, k]))
        first.append(pltpu.make_async_copy(write_in.at[k], write.at[k], sem_a.at[2, k]))
    for k in range(PEERS):
        t_in = ts_in[k].at[:, own] if k == 0 else ts_in[k]
        later[k].append(pltpu.make_async_copy(t_in, t.at[k], sem_a.at[3, k]))
        later[k].append(pltpu.make_async_copy(lead_in.at[k], lead.at[k], sem_a.at[4, k]))
        later[k].append(pltpu.make_async_copy(grid_in.at[k], grid.at[k], sem_g.at[k]))
    for c in first + sum(later, []):
        c.start()
    for c in first:
        c.wait()

    state[...] = jnp.zeros_like(state)
    for j in range(PEERS):
        k = place ^ j
        entry[k] = state[...].astype(BF)
        scaled[k] = (write[k].astype(F32) * x[k].astype(F32)).astype(BF)
        if j < PEERS - 1:
            state[...] = keep_ref[k] * state[...] + dot_tn(bc[k, :, :STATE], scaled[k])
    low = lax.broadcasted_iota(jnp.int32, (BLOCK, 2 * HEAD), 1) < HEAD

    def block(k, carry):
        for ref, sem in ((t, sem_a.at[3, k]), (lead, sem_a.at[4, k]), (grid, sem_g.at[k])):
            pltpu.make_async_copy(ref.at[k], ref.at[k], sem).wait()
        b_map = bc[k, :, :STATE]
        c_map = bc[k, :, STATE:]
        cross[...] = dot_nt(c_map, b_map)
        base[...] = (
            dot_nn(c_map, entry[k]) * lead[k].astype(F32) + skip_ref[...] * x[k].astype(F32) - t[k].astype(F32)
        )
        score[...] = jnp.zeros_like(score)
        weight = weight_ref[k]
        for p in range(LOCAL_HEADS // 2):
            at = slice(2 * HEAD * p, 2 * HEAD * (p + 1))
            xp = x[k, :, at]
            d0 = grid[k, 2 * p].astype(F32)
            d1 = grid[k, 2 * p + 1].astype(F32)
            m0 = (cross[...] * d0).astype(BF)
            m1 = (cross[...] * d1).astype(BF)
            y = jnp.where(low, dot_nn(m0, xp), dot_nn(m1, xp))
            og = (weight * (base[:, at] + y)).astype(BF)
            zero = jnp.zeros_like(og)
            g0 = dot_nt(jnp.where(low, og, zero), xp)
            g1 = dot_nt(jnp.where(low, zero, og), xp)
            score[...] += g0 * d0 + g1 * d1
            dx = jnp.where(low, dot_tn(m0, og), dot_tn(m1, og))
            ogf = og.astype(F32)
            acc[k, :, at] = dx + skip_ref[:, at] * ogf
            outs[:, at] = (lead[k, :, at].astype(F32) * ogf).astype(BF)
        sg = score[...].astype(BF)
        pull[k] = dot_tn(c_map, outs[...])
        ig[k, :, STATE:] = dot_nt(outs[...], entry[k]) + dot_nn(sg, b_map)
        ig[k, :, :STATE] = dot_tn(sg, c_map)
        return carry

    lax.fori_loop(0, PEERS, block, 0)

    state[...] = jnp.zeros_like(state)
    for j in reversed(range(PEERS)):
        k = place ^ j
        leave = state[...].astype(BF)
        acc[k] = acc[k] + write[k].astype(F32) * dot_nn(bc[k, :, :STATE], leave)
        ig[k, :, :STATE] += dot_nt(scaled[k], leave)
        if j > 0:
            state[...] = keep_ref[k] * state[...] + pull[k]
    for k in range(PEERS):
        vg_out[k][...] = acc[k].astype(BF)
        bg_out[k][...] = ig[k].astype(bg_out[k].dtype)


def layer(place, xs, ts, bcs, grid, lead, write, weight, keep, skip):
    return pl.pallas_call(
        layer_kernel,
        in_specs=[smem()] + [anywhere()] * 15 + [vmem()] * 3,
        out_specs=[vmem()] * 8,
        out_shape=[jax.ShapeDtypeStruct((BLOCK, WIDE), BF)] * 4
        + [jax.ShapeDtypeStruct((BLOCK, 2 * STATE), F32)]
        + [jax.ShapeDtypeStruct((BLOCK, 2 * STATE), BF)] * 3,
        scratch_shapes=[
            pltpu.VMEM((PEERS, BLOCK, WIDE), BF),
            pltpu.VMEM((PEERS, BLOCK, WIDE), BF),
            pltpu.VMEM((PEERS, BLOCK, 2 * STATE), BF),
            pltpu.VMEM((PEERS, LOCAL_HEADS, BLOCK, BLOCK), BF),
            pltpu.VMEM((PEERS, BLOCK, WIDE), BF),
            pltpu.VMEM((PEERS, BLOCK, WIDE), BF),
            pltpu.VMEM((PEERS, STATE, WIDE), BF),
            pltpu.VMEM((PEERS, STATE, WIDE), F32),
            pltpu.VMEM((PEERS, BLOCK, WIDE), BF),
            pltpu.VMEM((BLOCK, WIDE), BF),
            pltpu.VMEM((PEERS, BLOCK, WIDE), F32),
            pltpu.VMEM((STATE, WIDE), F32),
            pltpu.VMEM((BLOCK, WIDE), F32),
            pltpu.VMEM((BLOCK, BLOCK), F32),
            pltpu.VMEM((BLOCK, BLOCK), F32),
            pltpu.VMEM((PEERS, BLOCK, 2 * STATE), F32),
            pltpu.SemaphoreType.DMA((5, PEERS)),
            pltpu.SemaphoreType.DMA((PEERS,)),
        ],
        compiler_params=pltpu.CompilerParams(vmem_limit_bytes=56 * MIB),
        cost_estimate=pl.CostEstimate(flops=5_000_000_000, bytes_accessed=24_000_000, transcendentals=0),
        name="layer",
    )(place, *xs, *ts, *bcs, grid, lead, write, weight, keep, skip)


def gather_heads_kernel(place_ref, p0, p1, p2, p3, out_ref, sems):
    copies = []
    for k, piece in enumerate((p0, p1, p2, p3)):
        at = pl.multiple_of((place_ref[0] ^ k) * WIDE, WIDE)
        copies.append(pltpu.make_async_copy(piece, out_ref.at[:, pl.ds(at, WIDE)], sems.at[k]))
        copies[-1].start()
    for c in copies:
        c.wait()


def gather_heads(place, pieces):
    return pl.pallas_call(
        gather_heads_kernel,
        in_specs=[smem()] + [anywhere()] * 4,
        out_specs=vmem(),
        out_shape=jax.ShapeDtypeStruct((BLOCK, 4 * WIDE), BF),
        scratch_shapes=[pltpu.SemaphoreType.DMA((4,))],
        cost_estimate=pl.CostEstimate(flops=1000, bytes_accessed=4_200_000, transcendentals=0),
        name="gather_heads",
    )(place, *pieces)


def body(
    hidden_in,
    bc_weight,
    values,
    teacher,
    decay_codes,
    resets,
    head_decay_rates,
    skip_gain,
    confidence,
):
    me = lax.axis_index("seq")
    dp = lax.axis_index("dp")
    place = me.astype(jnp.int32).reshape(1)
    core = (dp % 2).astype(jnp.int32).reshape(1)
    chip = dp // 2
    distance = jnp.array([z * 4 + a for a in range(4) for z in ZREL], jnp.int32)
    order = (chip ^ distance).astype(jnp.int32)
    x_place = (chip % 4).astype(jnp.int32).reshape(1)
    turns = jnp.array([ZREL.index(z) for z in range(8)], jnp.int32)
    pos = turns[jnp.arange(8, dtype=jnp.int32) ^ (chip // 4)]
    doc_len = BLOCK * PEERS
    all_tokens = doc_len * 64

    aux = jnp.concatenate(
        [
            decay_codes.astype(BF).reshape(BLOCK, PEERS, LOCAL_HEADS),
            jnp.broadcast_to(resets.astype(BF)[:, None, None], (BLOCK, PEERS, 1)),
            jnp.broadcast_to(confidence.astype(BF)[:, None, None], (BLOCK, PEERS, 1)),
            jnp.zeros((BLOCK, PEERS, 128 - LOCAL_HEADS - 2), BF),
        ],
        axis=2,
    ).reshape(BLOCK, PEERS * 128)
    r = bc_weight[None]
    r = jnp.concatenate([r, over_dp(r, 32)], axis=0)
    cut = cut_heads(place, values, aux, teacher, r)
    v_cut, t_cut = cut[0:3], cut[3:6]
    x1, x3 = over_seq(v_cut[0], 1), over_seq(v_cut[2], 3)
    (far,) = after([v_cut[1]], [x1])
    xs = [values, x1, over_seq(far, 2), x3]

    facts = jnp.stack(
        [lax.dynamic_slice_in_dim(aux, me * 128, 128, axis=1)] + [x[:, WIDE:] for x in xs[1:]]
    ).astype(F32)
    base = jnp.log(0.9995 + 0.0004 * facts[:, :, :LOCAL_HEADS] / 15.0)
    rates = lax.dynamic_slice_in_dim(head_decay_rates, me * LOCAL_HEADS, LOCAL_HEADS)
    log_decay = (
        rates[None, None, :] * (1.0 + SPIKE_MULTIPLIER * facts[:, :, LOCAL_HEADS, None]) * base
    )
    lower = (
        lax.broadcasted_iota(jnp.int32, (BLOCK, BLOCK), 0)
        >= lax.broadcasted_iota(jnp.int32, (BLOCK, BLOCK), 1)
    ).astype(F32)
    cum_rows = jnp.swapaxes(
        jnp.einsum("ts,ksh->kth", lower, log_decay, precision=lax.Precision.HIGHEST), 1, 2
    )
    step_rows = jnp.swapaxes(-STEP_FACTOR * base, 1, 2)
    small = jnp.concatenate([cum_rows, step_rows], axis=1)
    grid, lead, write, decayed = decays(small)
    conf_all = facts[:, :, LOCAL_HEADS + 1]
    weight = (conf_all * doc_len / jnp.sum(conf_all))[:, :, None]
    keep = jnp.repeat(jnp.exp(small[:, :LOCAL_HEADS, BLOCK - 1]), HEAD, axis=1)[:, None, :]
    skip = jnp.repeat(
        lax.dynamic_slice_in_dim(skip_gain, me * LOCAL_HEADS, LOCAL_HEADS), HEAD
    )[None, :]

    r = jnp.concatenate([r] + [over_dp(r, m) for m in (16, 8, 24)], axis=0)
    own = [r] + [over_dp(r, 2 * a) for a in (1, 2, 3)]
    other = [over_dp(p, 1) for p in own]
    full_weight, rows = project(hidden_in, own, other, order, core, [xs[1], xs[3], decayed])
    near = after([t_cut[0], t_cut[2]], [rows])
    ts = [teacher, over_seq(near[0], 1), over_seq(t_cut[1], 2), over_seq(near[1], 3)]
    *hx, cut_done = split_hidden(x_place, hidden_in, r)
    bcs = [rows] + [over_seq(rows, k) for k in (1, 2, 3)]
    near = after([hx[1], hx[3]], [own[3]])
    hx1, hx3 = over_dp(near[0], 2), over_dp(near[1], 6)
    hx = [hx[0], hx1, over_dp(hx[2], 4), hx3]
    (bcs[0],) = after([bcs[0]], [hx1])

    outs = layer(place, xs, ts, bcs, grid, lead, write, weight, keep, skip)
    vgs, bgs = outs[:4], outs[4:]
    bc_grad = bgs[0]
    for k in (1, 2, 3):
        bc_grad = bc_grad + over_seq(bgs[k], k).astype(F32)
    bc_grad = bc_grad.astype(BF)
    pieces = [vgs[0]] + [over_seq(vgs[k], k) for k in (1, 2, 3)]

    bc_grads = jnp.concatenate([bc_grad] + [over_dp(bc_grad, 2 * a) for a in (1, 2, 3)], axis=0)
    turned = turn(pos, core, hx)
    send = dot_nn(turned[1].reshape(512, 4 * BLOCK), bc_grads).astype(BF)
    (send,) = after([send], [pieces[1], pieces[3]])
    total = dot_nn(turned[0].reshape(512, 4 * BLOCK), bc_grads)
    total = (total + over_dp(send, 1).astype(F32)).reshape(8, 64, 256)
    half = total.astype(BF)
    came = [over_dp(half[2:4], 16), over_dp(half[4:6], 8), over_dp(half[6:8], 24)]
    total = total[0:2]
    for c in came:
        total = total + c.astype(F32)
    (total,) = after([total], [pieces[2]])
    total = total[0] + over_dp(total[1].astype(BF), 32).astype(F32)

    hidden_grad = dot_nt(bc_grad, full_weight).astype(BF)
    values_grad = gather_heads(place, pieces)
    total = total + sum(over_seq(total, k) for k in (1, 2, 3))
    return values_grad, hidden_grad, total / math.sqrt(all_tokens)


def solution(mesh):
    return jax.shard_map(
        body,
        mesh=mesh,
        in_specs=(
            P(("dp", "seq"), None),
            P("dp", None),
            P(("dp", "seq"), None),
            P(("dp", "seq"), None),
            P(("dp", "seq"), None),
            P(("dp", "seq")),
            P(),
            P(),
            P(("dp", "seq")),
        ),
        out_specs=(P(("dp", "seq"), None), P(("dp", "seq"), None), P("dp", None)),
        check_vma=False,
    )
```
